32 devices in a mesh: dp: 8 (over y, x, core), feat: 4 (over z).
Axes of the slice: x: 2, y: 2, z: 4, core: 2. Of those that a mesh axis runs over, the one named last changes fastest.
Arguments:
- images: bfloat16 [2048, 3072], P(('dp', 'feat')), may hold values from -6 to 6
- labels: int32 [2048], P('dp'), may hold values from 0 to 999
- predictions: float32 [2048, 1000], P('dp'), may hold values from -2 to 2
- filters: bfloat16 [75, 512], P(None, 'feat'), may hold values from -0.75 to 0.75
- biases: float32 [512], P('feat'), may hold values from -3 to 3
Outputs:
- weights: float32 [2048, 1000], P('feat')
- new_residual: float32 [2048, 1000], P(('dp', 'feat'))
The draws below stay inside these ranges and needn't reach their ends.
All inputs are finite; a program needn't handle non-finite values.
Results may differ from the reference program's by a relative error of at most 0.007.
The reference program's roundings to bfloat16 on the way count: a program that leaves them out, or rounds other values in their place, can miss the bound.
Values may be sent and summed in bfloat16 or wider, within the bound.
A program may use at most 192 MiB of HBM per device.

```python
import jax
import jax.numpy as jnp
from jax import lax

SIDE = 32
CHAN = 3
KSIZE = 5
FILT = 128
CLASSES = 1000
FEATB = 512
IMAGES = 2048
BLOCKS = 4


def touch_ends(values, key, least, high):
    extent = values.shape
    place = [jax.random.randint(jax.random.fold_in(key, axis), (), 0, extent[axis]) for axis in range(len(extent))]
    values = values.at[tuple(place)].set(least)
    longest = extent.index(max(extent))
    place[longest] = (place[longest] + 1) % extent[longest]
    return values.at[tuple(place)].set(high)


def level_of(own_key, dims, pieces, low, high):
    level = 1.0
    for axis_at, blocks in pieces:
        draws = jax.random.uniform(jax.random.fold_in(jax.random.fold_in(own_key, 6), axis_at), (blocks,), jnp.float32, low / len(pieces), high / len(pieces))
        level = level * jnp.repeat(jnp.exp(draws), dims[axis_at] // blocks).reshape((-1,) + (1,) * (len(dims) - 1 - axis_at))
    return level


def noise(rng, extent, width, bound, cuts=(), kind=jnp.bfloat16):
    drawn = width * jax.random.normal(rng, extent, jnp.float32)
    if cuts:
        drawn = drawn * level_of(rng, extent, cuts, -0.22, 0.18)
    return jnp.clip(drawn, -bound, bound).astype(kind)


def setup_inputs(seed: int = 0) -> dict:
    key_of = jax.random.split(jax.random.key(seed), 6)
    images = noise(key_of[0], (IMAGES, SIDE * SIDE * CHAN), 1.0, 6.0, ((0, 32),))
    labels = touch_ends(jax.random.randint(key_of[1], (IMAGES,), 0, CLASSES), jax.random.fold_in(key_of[1], 1), 0, CLASSES - 1).astype(jnp.int32)
    predictions = noise(key_of[2], (IMAGES, CLASSES), 0.3, 2.0, ((0, 8),), jnp.float32)
    filters = noise(key_of[3], (KSIZE * KSIZE * CHAN, BLOCKS * FILT), (KSIZE * KSIZE * CHAN) ** -0.5, 0.75, ((1, 4),))
    biases = noise(key_of[4], (BLOCKS * FILT,), 0.5, 3.0, ((0, 4),), jnp.float32)
    return dict(images=images, labels=labels, predictions=predictions, filters=filters, biases=biases)


def chol_solve(factor, rhs):
    middle = lax.linalg.triangular_solve(factor, rhs, left_side=True, lower=True, transpose_a=False)
    return lax.linalg.triangular_solve(factor, middle, left_side=True, lower=True, transpose_a=True)

def split_parts(values):
    upper = values.astype(jnp.bfloat16)
    lower = (values - upper.astype(jnp.float32)).astype(jnp.bfloat16)
    return (upper, lower)

def left_product(feats, other):
    return lax.dot_general(feats.astype(jnp.float32), other.astype(jnp.float32), (((0,), (0,)), ((), ())), preferred_element_type=jnp.float32)

def conv_pool(imgs, kernel, offsets):
    count = imgs.shape[0]
    pics = imgs.reshape(count, SIDE, SIDE, CHAN)
    response = lax.conv_general_dilated(pics, kernel, (1, 1), 'VALID', dimension_numbers=('NHWC', 'HWIO', 'NHWC'), preferred_element_type=jnp.float32)
    response = jnp.maximum(response + offsets, 0.0)
    half = (SIDE - KSIZE + 1) // 2
    pooled = response.reshape(count, 2, half, 2, half, FILT).mean(axis=(2, 4))
    return jnp.transpose(pooled, (0, 3, 1, 2)).reshape(count, 4 * FILT).astype(jnp.bfloat16)

def reference(images, labels, predictions, filters, biases):
    residual = (labels[:, None] == jnp.arange(CLASSES, dtype=jnp.int32)[None, :]).astype(jnp.float32) - predictions
    res_upper, res_lower = split_parts(residual)
    group = 16

    def one_block(index):
        kernel = lax.dynamic_slice_in_dim(filters, index * FILT, FILT, 1).reshape(KSIZE, KSIZE, CHAN, FILT)
        offsets = lax.dynamic_slice_in_dim(biases, index * FILT, FILT, 0)
        blocks = images.reshape(IMAGES // group, group, SIDE * SIDE * CHAN)
        feats = lax.map(lambda part: conv_pool(part, kernel, offsets), blocks).reshape(IMAGES, FEATB)
        gram = left_product(feats, feats)
        gram = gram / IMAGES + 0.5 * jnp.eye(FEATB, dtype=jnp.float32)
        cross = (left_product(feats, res_upper) + left_product(feats, res_lower)) / IMAGES
        factor = jnp.linalg.cholesky(gram)
        solved = chol_solve(factor, cross)
        sol_upper, sol_lower = split_parts(solved)
        fit = jnp.dot(feats.astype(jnp.float32), sol_upper.astype(jnp.float32), preferred_element_type=jnp.float32) + jnp.dot(feats.astype(jnp.float32), sol_lower.astype(jnp.float32), preferred_element_type=jnp.float32)
        return (solved, fit)

    def step(total, index):
        solved, fit = one_block(index)
        return (total + fit, solved)
    total, solved_all = lax.scan(step, jnp.zeros((IMAGES, CLASSES), jnp.float32), jnp.arange(BLOCKS, dtype=jnp.int32))
    return (solved_all.reshape(BLOCKS * FEATB, CLASSES), residual - total)
```

```python
import functools

import jax
import jax.numpy as jnp
import ml_dtypes
import numpy as np
from jax import lax
from jax.experimental import pallas as pl
from jax.experimental.pallas import tpu as pltpu
from jax.sharding import PartitionSpec as P

SIDE = 32
CHAN = 3
KSIZE = 5
MAP = SIDE - KSIZE + 1
HALF = MAP // 2
TALL, WIDE = 2, 7
WROWS, WCOLS = TALL + KSIZE - 1, (WIDE + KSIZE - 1) * CHAN
TAPS = KSIZE * KSIZE * CHAN
OUTS = TALL * WIDE
DEPTH = 256
SPAN = 640
WIN = (HALF // TALL) * (HALF // WIDE)
EXT = 80


def window_picks():
    picks = np.zeros((MAP // WIDE, 2, SPAN, DEPTH), ml_dtypes.bfloat16)
    for g in range(MAP // WIDE):
        for par in range(2):
            for row in range(WROWS):
                for t in range(WCOLS):
                    picks[g, par, par * 64 + row * SIDE * CHAN + g * WIDE * CHAN + t, row * WCOLS + t] = 1
    return picks


def tap_picks():
    picks = np.zeros((OUTS, DEPTH, EXT), ml_dtypes.bfloat16)
    for a in range(TALL):
        for b in range(WIDE):
            for d in range(KSIZE):
                for t in range(KSIZE * CHAN):
                    picks[a * WIDE + b, (a + d) * WCOLS + b * CHAN + t, d * KSIZE * CHAN + t] = 1
            for extra in range(3):
                picks[a * WIDE + b, WROWS * WCOLS + extra, TAPS + extra] = 1
    return picks


def order_picks(filt):
    picks = np.zeros((4 * filt, 4 * filt), ml_dtypes.bfloat16)
    for q in range(4):
        for f in range(filt):
            picks[q * filt + f, f * 4 + q] = 1
    return picks


def conv_kernel(x_ref, fb_ref, wp_ref, tp_ref, op_ref, out_ref, left, band, quad):
    count = x_ref.shape[0]
    blocks = out_ref.shape[0]
    filt = out_ref.shape[2] // 4
    half_rows = HALF // TALL

    def make_band(o, carry):
        band[o] = jnp.dot(tp_ref[o], fb_ref[...], preferred_element_type=jnp.float32).astype(jnp.bfloat16)
        return carry

    lax.fori_loop(0, OUTS, make_band, 0)
    lanes = lax.broadcasted_iota(jnp.int32, (1, DEPTH), 1)
    ones = jnp.where((lanes >= WROWS * WCOLS) & (lanes < WROWS * WCOLS + 3), 1.0, 0.0)
    for g in range(MAP // WIDE):
        for par in range(2):
            for k in range(half_rows):
                start = 384 * k + 128 * par
                win = jnp.dot(x_ref[:, start : start + SPAN], wp_ref[g, par], preferred_element_type=jnp.float32)
                i2 = 2 * k + par
                q = (i2 // half_rows) * 2 + g // 2
                slot = (i2 % half_rows) * 2 + g % 2
                left[q, slot * count : (slot + 1) * count, :] = (win + ones).astype(jnp.bfloat16)
    for n in range(blocks // 2):
        for q in range(4):

            def one(o, acc):
                resp = jnp.dot(
                    left[q], band[o, :, n * 2 * filt : (n + 1) * 2 * filt], preferred_element_type=jnp.float32
                )
                resp = jnp.maximum(resp, 0.0)
                return acc + resp.reshape(WIN, count, 2 * filt).sum(axis=0)

            acc = lax.fori_loop(0, OUTS, one, jnp.zeros((count, 2 * filt), jnp.float32))
            acc = (acc / (HALF * HALF)).astype(jnp.bfloat16)
            for h in range(2):
                quad[2 * n + h, :, q * filt : (q + 1) * filt] = acc[:, h * filt : (h + 1) * filt]
    for b in range(blocks):
        out_ref[b] = jnp.dot(quad[b], op_ref[...], preferred_element_type=jnp.float32).astype(jnp.bfloat16)


def conv_feats(images, bank):
    count = images.shape[0]
    filt = 128
    blocks = bank.shape[1] // filt
    vmem = pl.BlockSpec(memory_space=pltpu.VMEM)
    return pl.pallas_call(
        conv_kernel,
        out_shape=jax.ShapeDtypeStruct((blocks, count, 4 * filt), jnp.bfloat16),
        in_specs=[vmem] * 5,
        out_specs=vmem,
        scratch_shapes=[
            pltpu.VMEM((4, WIN * count, DEPTH), jnp.bfloat16),
            pltpu.VMEM((OUTS, DEPTH, blocks * filt), jnp.bfloat16),
            pltpu.VMEM((blocks, count, 4 * filt), jnp.bfloat16),
        ],
        compiler_params=pltpu.CompilerParams(vmem_limit_bytes=48 * 2**20),
    )(images, bank, window_picks(), tap_picks(), order_picks(filt))


def invert_block(rows):
    slabs = len(rows)
    lane = lax.broadcasted_iota(jnp.int32, (8, 128), 1)
    sub = lax.broadcasted_iota(jnp.int32, (8, 128), 0)
    for step in range(slabs * 2):
        k = 4 * step
        t, off = k // 8, k % 8
        own = rows[t]
        r = [jnp.broadcast_to(own[off + i : off + i + 1, :], (8, 128)) for i in range(4)]
        a = [[None] * 4 for _ in range(4)]
        for i in range(4):
            for j in range(i, 4):
                a[i][j] = jnp.broadcast_to(r[i][:, k + j : k + j + 1], (8, 128))
        inv = 1.0 / (a[0][0] * a[1][1] - a[0][1] * a[0][1])
        p00, p01, p11 = a[1][1] * inv, -a[0][1] * inv, a[0][0] * inv
        u00 = p00 * a[0][2] + p01 * a[1][2]
        u01 = p00 * a[0][3] + p01 * a[1][3]
        u10 = p01 * a[0][2] + p11 * a[1][2]
        u11 = p01 * a[0][3] + p11 * a[1][3]
        s00 = a[2][2] - (a[0][2] * u00 + a[1][2] * u10)
        s01 = a[2][3] - (a[0][2] * u01 + a[1][2] * u11)
        s11 = a[3][3] - (a[0][3] * u01 + a[1][3] * u11)
        sinv = 1.0 / (s00 * s11 - s01 * s01)
        q00, q01, q11 = s11 * sinv, -s01 * sinv, s00 * sinv
        v00 = u00 * q00 + u01 * q01
        v01 = u00 * q01 + u01 * q11
        v10 = u10 * q00 + u11 * q01
        v11 = u10 * q01 + u11 * q11
        d = [
            [p00 + v00 * u00 + v01 * u01, p01 + v00 * u10 + v01 * u11, -v00, -v01],
            [None, p11 + v10 * u10 + v11 * u11, -v10, -v11],
            [None, None, q00, q01],
            [None, None, None, q11],
        ]
        for i in range(4):
            for j in range(i):
                d[i][j] = d[j][i]
        inside = (lane >= k) & (lane < k + 4)
        rt = [jnp.where(inside, jnp.where(lane == k + i, 1.0, 0.0), r[i]) for i in range(4)]
        new = [d[i][0] * rt[0] + d[i][1] * rt[1] + d[i][2] * rt[2] + d[i][3] * rt[3] for i in range(4)]
        out = []
        for s in range(slabs):
            c = [jnp.broadcast_to(rows[s][:, k + i : k + i + 1], (8, 128)) for i in range(4)]
            base = jnp.where(inside, 0.0, rows[s])
            val = base - (c[0] * new[0] + c[1] * new[1]) - (c[2] * new[2] + c[3] * new[3])
            if s == t:
                for i in range(4):
                    val = jnp.where(sub == off + i, new[i], val)
            out.append(val)
        rows = out
    return rows


def dot32(a, b, dims=((1,), (0,))):
    return lax.dot_general(a, b, (dims, ((), ())), precision=lax.Precision.HIGHEST, preferred_element_type=jnp.float32)


def solve_kernel(total, gram_ref, cross_ref, out_ref, mat, diag, upper):
    size = gram_ref.shape[0]
    steps = size // 128
    row = lax.broadcasted_iota(jnp.int32, (size, size), 0)
    col = lax.broadcasted_iota(jnp.int32, (size, size), 1)
    mat[...] = gram_ref[...] / total + jnp.where(row == col, 0.5, 0.0)
    out_ref[...] = cross_ref[...] / total
    for k in range(steps):
        lo, hi = 128 * k, 128 * (k + 1)
        rows = invert_block([mat[lo + 8 * s : lo + 8 * s + 8, lo:hi] for s in range(16)])
        inv = jnp.concatenate(rows, axis=0)
        diag[k] = inv
        if hi < size:
            side = mat[lo:hi, hi:]
            ratio = dot32(inv, side)
            upper[lo:hi, hi:] = ratio
            mat[hi:, hi:] = mat[hi:, hi:] - dot32(side, ratio, ((0,), (0,)))
            out_ref[hi:, :] = out_ref[hi:, :] - dot32(ratio, out_ref[lo:hi, :], ((0,), (0,)))
    for k in reversed(range(steps)):
        lo, hi = 128 * k, 128 * (k + 1)
        val = dot32(diag[k], out_ref[lo:hi, :])
        if hi < size:
            val = val - dot32(upper[lo:hi, hi:], out_ref[hi:, :])
        out_ref[lo:hi, :] = val


def ridge_solve(gram, cross, total):
    size = gram.shape[0]
    vmem = pl.BlockSpec(memory_space=pltpu.VMEM)
    return pl.pallas_call(
        functools.partial(solve_kernel, total),
        out_shape=jax.ShapeDtypeStruct(cross.shape, jnp.float32),
        in_specs=[vmem] * 2,
        out_specs=vmem,
        scratch_shapes=[
            pltpu.VMEM((size, size), jnp.float32),
            pltpu.VMEM((size // 128, 128, 128), jnp.float32),
            pltpu.VMEM((size, size), jnp.float32),
        ],
        compiler_params=pltpu.CompilerParams(vmem_limit_bytes=48 * 2**20),
    )(gram, cross)


def split_parts(values):
    upper = lax.reduce_precision(values, 8, 7)
    lower = lax.reduce_precision(values - upper, 8, 7)
    return (upper.astype(jnp.bfloat16), lower.astype(jnp.bfloat16))


def left_product(feats, other):
    return lax.dot_general(feats, other, (((0,), (0,)), ((), ())), preferred_element_type=jnp.float32)


def filter_rows(filters, biases):
    first = lax.reduce_precision(biases, 8, 7)
    second = lax.reduce_precision(biases - first, 8, 7)
    extra = jnp.stack([first, second, biases - first - second]).astype(jnp.bfloat16)
    fill = jnp.zeros((EXT - TAPS - 3, filters.shape[1]), jnp.bfloat16)
    return jnp.concatenate([filters, extra, fill], axis=0)


def shards(images, labels, predictions, filters, biases):
    share = images.shape[0]
    total_images = share * lax.axis_size("feat") * lax.axis_size("dp")
    bank = lax.all_gather(filter_rows(filters, biases), "feat", axis=1, tiled=True)
    own = conv_feats(images, bank)
    feats = lax.all_to_all(own, "feat", split_axis=0, concat_axis=0, tiled=True)
    feats = feats.reshape(feats.shape[0] * share, feats.shape[2])
    residual = (
        labels[:, None] == jnp.arange(predictions.shape[1], dtype=jnp.int32)[None, :]
    ).astype(jnp.float32) - predictions
    res_upper, res_lower = split_parts(residual)
    gram = left_product(feats, feats)
    cross = left_product(feats, res_upper) + left_product(feats, res_lower)
    gram, cross = lax.psum((gram, cross), "dp")
    solved = ridge_solve(gram, cross, total_images)
    sol_upper, sol_lower = split_parts(solved)
    fitted = lax.psum_scatter(
        (
            jnp.dot(feats, sol_upper, preferred_element_type=jnp.float32)
            + jnp.dot(feats, sol_lower, preferred_element_type=jnp.float32)
        ).astype(jnp.bfloat16),
        "feat",
        scatter_dimension=0,
        tiled=True,
    ).astype(jnp.float32)
    mine = lax.dynamic_slice_in_dim(residual, lax.axis_index("feat") * share, share, 0)
    return (solved, mine - fitted)


def solution(mesh):
    placed = (P(("dp", "feat"), None), P("dp"), P("dp", None), P(None, "feat"), P("feat"))
    return jax.shard_map(
        shards,
        mesh=mesh,
        in_specs=placed,
        out_specs=(P("feat", None), P(("dp", "feat"), None)),
        check_vma=False,
    )
```

```python
import functools

import jax
import jax.numpy as jnp
import ml_dtypes
import numpy as np
from jax import lax
from jax.experimental import pallas as pl
from jax.experimental.pallas import tpu as pltpu
from jax.sharding import PartitionSpec as P

SIDE = 32
CHAN = 3
KSIZE = 5
MAP = SIDE - KSIZE + 1
HALF = MAP // 2
TALL, WIDE = 2, 7
WROWS, WCOLS = TALL + KSIZE - 1, (WIDE + KSIZE - 1) * CHAN
TAPS = KSIZE * KSIZE * CHAN
OUTS = TALL * WIDE
DEPTH = 256
SPAN = 640
WIN = (HALF // TALL) * (HALF // WIDE)
EXT = 80


def window_picks():
    picks = np.zeros((MAP // WIDE, 2, SPAN, DEPTH), ml_dtypes.bfloat16)
    for g in range(MAP // WIDE):
        for par in range(2):
            for row in range(WROWS):
                for t in range(WCOLS):
                    picks[g, par, par * 64 + row * SIDE * CHAN + g * WIDE * CHAN + t, row * WCOLS + t] = 1
    return picks


def tap_picks():
    picks = np.zeros((OUTS, DEPTH, EXT), ml_dtypes.bfloat16)
    for a in range(TALL):
        for b in range(WIDE):
            for d in range(KSIZE):
                for t in range(KSIZE * CHAN):
                    picks[a * WIDE + b, (a + d) * WCOLS + b * CHAN + t, d * KSIZE * CHAN + t] = 1
            for extra in range(3):
                picks[a * WIDE + b, WROWS * WCOLS + extra, TAPS + extra] = 1
    return picks


def order_picks(filt):
    picks = np.zeros((4 * filt, 4 * filt), ml_dtypes.bfloat16)
    for q in range(4):
        for f in range(filt):
            picks[q * filt + f, f * 4 + q] = 1
    return picks


def conv_kernel(x_ref, fb_ref, wp_ref, tp_ref, op_ref, out_ref, left, band, quad):
    count = x_ref.shape[0]
    blocks = out_ref.shape[0]
    filt = out_ref.shape[2] // 4
    half_rows = HALF // TALL

    def make_band(o, carry):
        band[o] = jnp.dot(tp_ref[o], fb_ref[...], preferred_element_type=jnp.float32).astype(jnp.bfloat16)
        return carry

    lax.fori_loop(0, OUTS, make_band, 0)
    lanes = lax.broadcasted_iota(jnp.int32, (1, DEPTH), 1)
    ones = jnp.where((lanes >= WROWS * WCOLS) & (lanes < WROWS * WCOLS + 3), 1.0, 0.0)
    for g in range(MAP // WIDE):
        for par in range(2):
            for k in range(half_rows):
                start = 384 * k + 128 * par
                win = jnp.dot(x_ref[:, start : start + SPAN], wp_ref[g, par], preferred_element_type=jnp.float32)
                i2 = 2 * k + par
                q = (i2 // half_rows) * 2 + g // 2
                slot = (i2 % half_rows) * 2 + g % 2
                left[q, slot * count : (slot + 1) * count, :] = (win + ones).astype(jnp.bfloat16)
    for n in range(blocks // 2):
        for q in range(4):

            def some(step, acc):
                for part in range(TALL):
                    o = step * TALL + part
                    resp = jnp.dot(
                        left[q], band[o, :, n * 2 * filt : (n + 1) * 2 * filt], preferred_element_type=jnp.float32
                    )
                    resp = jnp.maximum(resp, 0.0)
                    acc = acc + resp.reshape(WIN, count, 2 * filt).sum(axis=0)
                return acc

            acc = lax.fori_loop(0, WIDE, some, jnp.zeros((count, 2 * filt), jnp.float32))
            acc = (acc / (HALF * HALF)).astype(jnp.bfloat16)
            for h in range(2):
                quad[2 * n + h, :, q * filt : (q + 1) * filt] = acc[:, h * filt : (h + 1) * filt]
    for b in range(blocks):
        out_ref[b] = jnp.dot(quad[b], op_ref[...], preferred_element_type=jnp.float32).astype(jnp.bfloat16)


def conv_feats(images, bank):
    count = images.shape[0]
    filt = 128
    blocks = bank.shape[1] // filt
    vmem = pl.BlockSpec(memory_space=pltpu.VMEM)
    return pl.pallas_call(
        conv_kernel,
        out_shape=jax.ShapeDtypeStruct((blocks, count, 4 * filt), jnp.bfloat16),
        in_specs=[vmem] * 5,
        out_specs=vmem,
        scratch_shapes=[
            pltpu.VMEM((4, WIN * count, DEPTH), jnp.bfloat16),
            pltpu.VMEM((OUTS, DEPTH, blocks * filt), jnp.bfloat16),
            pltpu.VMEM((blocks, count, 4 * filt), jnp.bfloat16),
        ],
        compiler_params=pltpu.CompilerParams(vmem_limit_bytes=48 * 2**20),
    )(images, bank, window_picks(), tap_picks(), order_picks(filt))


def invert_block(rows):
    slabs = len(rows)
    lane = lax.broadcasted_iota(jnp.int32, (8, 128), 1)
    sub = lax.broadcasted_iota(jnp.int32, (8, 128), 0)
    for step in range(slabs * 2):
        k = 4 * step
        t, off = k // 8, k % 8
        own = rows[t]
        r = [jnp.broadcast_to(own[off + i : off + i + 1, :], (8, 128)) for i in range(4)]
        a = [[None] * 4 for _ in range(4)]
        for i in range(4):
            for j in range(i, 4):
                a[i][j] = jnp.broadcast_to(r[i][:, k + j : k + j + 1], (8, 128))
        inv = 1.0 / (a[0][0] * a[1][1] - a[0][1] * a[0][1])
        p00, p01, p11 = a[1][1] * inv, -a[0][1] * inv, a[0][0] * inv
        u00 = p00 * a[0][2] + p01 * a[1][2]
        u01 = p00 * a[0][3] + p01 * a[1][3]
        u10 = p01 * a[0][2] + p11 * a[1][2]
        u11 = p01 * a[0][3] + p11 * a[1][3]
        s00 = a[2][2] - (a[0][2] * u00 + a[1][2] * u10)
        s01 = a[2][3] - (a[0][2] * u01 + a[1][2] * u11)
        s11 = a[3][3] - (a[0][3] * u01 + a[1][3] * u11)
        sinv = 1.0 / (s00 * s11 - s01 * s01)
        q00, q01, q11 = s11 * sinv, -s01 * sinv, s00 * sinv
        v00 = u00 * q00 + u01 * q01
        v01 = u00 * q01 + u01 * q11
        v10 = u10 * q00 + u11 * q01
        v11 = u10 * q01 + u11 * q11
        d = [
            [p00 + v00 * u00 + v01 * u01, p01 + v00 * u10 + v01 * u11, -v00, -v01],
            [None, p11 + v10 * u10 + v11 * u11, -v10, -v11],
            [None, None, q00, q01],
            [None, None, None, q11],
        ]
        for i in range(4):
            for j in range(i):
                d[i][j] = d[j][i]
        inside = (lane >= k) & (lane < k + 4)
        rt = [jnp.where(inside, jnp.where(lane == k + i, 1.0, 0.0), r[i]) for i in range(4)]
        new = [d[i][0] * rt[0] + d[i][1] * rt[1] + d[i][2] * rt[2] + d[i][3] * rt[3] for i in range(4)]
        out = []
        for s in range(slabs):
            c = [jnp.broadcast_to(rows[s][:, k + i : k + i + 1], (8, 128)) for i in range(4)]
            base = jnp.where(inside, 0.0, rows[s])
            val = base - (c[0] * new[0] + c[1] * new[1]) - (c[2] * new[2] + c[3] * new[3])
            if s == t:
                for i in range(4):
                    val = jnp.where(sub == off + i, new[i], val)
            out.append(val)
        rows = out
    return rows


def dot32(a, b, dims=((1,), (0,))):
    return lax.dot_general(a, b, (dims, ((), ())), precision=lax.Precision.HIGHEST, preferred_element_type=jnp.float32)


def solve_kernel(total, top_ref, corner_ref, cross_ref, out_ref, mat, diag, upper):
    size = cross_ref.shape[0]
    half = size // 2
    steps = size // 128
    row = lax.broadcasted_iota(jnp.int32, (size, size), 0)
    col = lax.broadcasted_iota(jnp.int32, (size, size), 1)
    mat[...] = jnp.where(row == col, 0.5, 0.0)
    mat[:half, :] = mat[:half, :] + top_ref[...] / total
    mat[half:, half:] = mat[half:, half:] + corner_ref[...] / total
    out_ref[...] = cross_ref[...] / total
    for k in range(steps):
        lo, hi = 128 * k, 128 * (k + 1)
        rows = invert_block([mat[lo + 8 * s : lo + 8 * s + 8, lo:hi] for s in range(16)])
        inv = jnp.concatenate(rows, axis=0)
        diag[k] = inv
        if hi < size:
            side = mat[lo:hi, hi:]
            ratio = dot32(inv, side)
            upper[lo:hi, hi:] = ratio
            mat[hi:, hi:] = mat[hi:, hi:] - dot32(side, ratio, ((0,), (0,)))
            out_ref[hi:, :] = out_ref[hi:, :] - dot32(ratio, out_ref[lo:hi, :], ((0,), (0,)))
    for k in reversed(range(steps)):
        lo, hi = 128 * k, 128 * (k + 1)
        val = dot32(diag[k], out_ref[lo:hi, :])
        if hi < size:
            val = val - dot32(upper[lo:hi, hi:], out_ref[hi:, :])
        out_ref[lo:hi, :] = val


def ridge_solve(top, corner, cross, total):
    size = cross.shape[0]
    vmem = pl.BlockSpec(memory_space=pltpu.VMEM)
    return pl.pallas_call(
        functools.partial(solve_kernel, total),
        out_shape=jax.ShapeDtypeStruct(cross.shape, jnp.float32),
        in_specs=[vmem] * 3,
        out_specs=vmem,
        scratch_shapes=[
            pltpu.VMEM((size, size), jnp.float32),
            pltpu.VMEM((size // 128, 128, 128), jnp.float32),
            pltpu.VMEM((size, size), jnp.float32),
        ],
        compiler_params=pltpu.CompilerParams(vmem_limit_bytes=48 * 2**20),
    )(top, corner, cross)


def split_parts(values):
    upper = lax.reduce_precision(values, 8, 7)
    lower = lax.reduce_precision(values - upper, 8, 7)
    return (upper.astype(jnp.bfloat16), lower.astype(jnp.bfloat16))


def left_product(feats, other):
    return lax.dot_general(feats, other, (((0,), (0,)), ((), ())), preferred_element_type=jnp.float32)


def filter_rows(filters, biases):
    first = lax.reduce_precision(biases, 8, 7)
    second = lax.reduce_precision(biases - first, 8, 7)
    extra = jnp.stack([first, second, biases - first - second]).astype(jnp.bfloat16)
    fill = jnp.zeros((EXT - TAPS - 3, filters.shape[1]), jnp.bfloat16)
    return jnp.concatenate([filters, extra, fill], axis=0)


def shards(images, labels, predictions, filters, biases):
    share = images.shape[0]
    total_images = share * lax.axis_size("feat") * lax.axis_size("dp")
    bank = lax.all_gather(filter_rows(filters, biases), "feat", axis=1, tiled=True)
    own = conv_feats(images, bank)
    feats = lax.all_to_all(own, "feat", split_axis=0, concat_axis=0, tiled=True)
    feats = feats.reshape(feats.shape[0] * share, feats.shape[2])
    residual = (
        labels[:, None] == jnp.arange(predictions.shape[1], dtype=jnp.int32)[None, :]
    ).astype(jnp.float32) - predictions
    res_upper, res_lower = split_parts(residual)
    half = feats.shape[1] // 2
    top = left_product(feats[:, :half], feats)
    corner = left_product(feats[:, half:], feats[:, half:])
    cross = left_product(feats, res_upper) + left_product(feats, res_lower)
    top, corner, cross = lax.psum((top, corner, cross), "dp")
    solved = ridge_solve(top, corner, cross, total_images)
    sol_upper, sol_lower = split_parts(solved)
    fitted = (
        (
            jnp.dot(feats, sol_upper, preferred_element_type=jnp.float32)
            + jnp.dot(feats, sol_lower, preferred_element_type=jnp.float32)
        ).astype(jnp.bfloat16)
    )
    parts = lax.all_to_all(fitted, "feat", split_axis=0, concat_axis=0, tiled=True)
    fitted = parts.reshape(-1, share, parts.shape[1]).astype(jnp.float32).sum(axis=0)
    mine = lax.dynamic_slice_in_dim(residual, lax.axis_index("feat") * share, share, 0)
    return (solved, mine - fitted)


def solution(mesh):
    placed = (P(("dp", "feat"), None), P("dp"), P("dp", None), P(None, "feat"), P("feat"))
    return jax.shard_map(
        shards,
        mesh=mesh,
        in_specs=placed,
        out_specs=(P("feat", None), P(("dp", "feat"), None)),
        check_vma=False,
    )
```
